256 devices in a mesh: blk: 128 (over z, x_lo, y, core), seg: 2 (over x_hi).
Axes of the slice: x: 4 (x_hi: 2, x_lo: 2; x = x_hi * 2 + x_lo), y: 4, z: 8, core: 2. Of those that a mesh axis runs over, the one named last changes fastest.
Arguments:
- recording: bfloat16 [2, 5120, 16384], P('seg', 'blk'), may hold values from -6 to 6
- filter_taps: float32 [31], replicated, may hold values from -1 to 1
- pair_offsets: int32 [128, 2], P('blk'), may hold values from 0 to 3, all different within a row
Outputs:
- correlations: bfloat16 [128, 2, 128, 200, 128], P('blk', None, None, 'seg')
The draws below stay inside these ranges and needn't reach their ends.
Inputs may be any that keep to these rules, and one draw needn't show every extreme that they name: `pair_offsets`: each row holds 2 different offsets, and every offset below 4 appears in some row.
All inputs are finite; a program needn't handle non-finite values.
Results may differ from the reference program's by a relative error of at most 0.0056.
Values may be sent and summed in bfloat16 or wider, within the bound.
No kernel may reach another device: no remote copies, remote signals or barrier semaphores. Data moves between devices by JAX's collectives and lax.ppermute only.
A program may use at most 192 MiB of HBM per device.

```python
import math
import jax
import jax.numpy as jnp
from jax import lax

CB = 128
BLOCKS = 128
CHANNELS = 16384
DECIM = 5
FILT = 31
TRS = 5120
TS = 1024
TIME = 2048
MAXLAG = 100
LAGS = 200
LAG_BLOCK = 25
BAND = 4
SLOTS = 2
N_SEG = 2


def levels(own_key, shape, split, smallest, largest):
    level = 1.0
    for position, shards_of in split:
        heights = jax.random.uniform(jax.random.fold_in(jax.random.fold_in(own_key, 6), position), (shards_of,), jnp.float32, smallest / len(split), largest / len(split))
        level = level * jnp.repeat(jnp.exp(heights), shape[position] // shards_of).reshape((-1,) + (1,) * (len(shape) - 1 - position))
    return level


def choose_distinct(rng, rows, number_of, top, lift):
    ranking = jax.random.permutation(jax.random.fold_in(rng, 1), number_of)
    favour = ranking
    for power in range(3):
        favour = favour * favour // number_of
    favour = favour * lift // number_of
    tickets = jax.random.randint(jax.random.fold_in(rng, 2), (rows, number_of), 0, 4096) + favour
    fixed_rows = jax.random.permutation(jax.random.fold_in(rng, 3), rows)[jnp.arange(number_of) % rows]
    tickets = jnp.where(jnp.arange(rows)[:, None] == fixed_rows[None, :], 1 << 14, tickets)
    priority = tickets * number_of + jnp.arange(number_of)
    return lax.top_k(priority.astype(jnp.int32), top)[1].astype(jnp.int32)


def noise(own_key, extent, scale, most, pieces=(), held_as=jnp.bfloat16):
    factor_of = levels(own_key, extent, pieces, -0.22, 0.18) if pieces else 1.0
    array = jax.random.normal(own_key, extent, jnp.float32) * scale * factor_of
    return jnp.minimum(jnp.maximum(array, -most), most).astype(held_as)


def setup_inputs(seed: int = 0) -> dict:
    arg_keys = jax.random.split(jax.random.key(seed), 4)
    return {
        "recording": noise(arg_keys[0], (N_SEG, TRS, CHANNELS), 1.0, 6.0, ((0, 2), (1, 128))),
        "filter_taps": noise(arg_keys[1], (FILT,), FILT ** -0.5, 1.0, (), jnp.float32),
        "pair_offsets": choose_distinct(arg_keys[2], BLOCKS, BAND, SLOTS, 0),
    }


def condition(segment, filter_taps):
    length = segment.shape[0]
    sample_count = length // DECIM
    groups = -(-FILT // DECIM)
    half_taps = FILT // 2
    zero_padded_length = DECIM * (sample_count + groups)
    padded = jnp.pad(segment.astype(jnp.float32), ((half_taps, zero_padded_length - half_taps - length), (0, 0)))
    stacked = padded.reshape(sample_count + groups, DECIM, segment.shape[1])
    weights = jnp.pad(filter_taps, (0, DECIM * groups - FILT)).reshape(groups, DECIM)
    filtered = jnp.zeros((sample_count, segment.shape[1]), jnp.float32)
    for group_index in range(groups):
        filtered = filtered + jnp.einsum('mpc,p->mc', stacked[group_index:group_index + sample_count], weights[group_index], precision=lax.Precision.HIGHEST)
    spread = jnp.sqrt(lax.optimization_barrier(jnp.mean(filtered * filtered, axis=0)) + 1e-06)
    return (filtered / spread).astype(jnp.bfloat16)

def lag_products(left_channel_block, right_block, first_lag, lag_count):
    length = left_channel_block.shape[1]
    padded = jnp.pad(right_block, ((0, 0), (MAXLAG, MAXLAG), (0, 0)))
    left_widened = left_channel_block.astype(jnp.float32)

    def single_channel_block(block_start):
        lag_index = block_start + jnp.arange(LAG_BLOCK, dtype=jnp.int32)
        window_frames = jax.vmap(lambda shift_at: lax.dynamic_slice_in_dim(padded, shift_at, length, 1))(lag_index)
        return jnp.einsum('vum,ivuq->miq', left_widened, window_frames.astype(jnp.float32))
    block_starts = (first_lag + jnp.arange(0, lag_count, LAG_BLOCK, dtype=jnp.int32)).astype(jnp.int32)
    lag_blocks = lax.map(single_channel_block, block_starts)
    return jnp.moveaxis(lag_blocks, 0, 1).reshape(left_channel_block.shape[2], lag_count, right_block.shape[2])

def reference(recording, filter_taps, pair_offsets):
    unit_norm_series = jnp.stack([condition(recording[segment_index], filter_taps) for segment_index in range(N_SEG)])
    by_block = unit_norm_series.reshape(N_SEG, TS, BLOCKS, CB)

    def single_owner_rows(owner_block):
        left_channel_block = lax.dynamic_index_in_dim(by_block, owner_block, 2, keepdims=False)
        slot_results = []
        for slot_index in range(SLOTS):
            partner = ((owner_block + pair_offsets[owner_block, slot_index]) % BLOCKS).astype(jnp.int32)
            right_block = lax.dynamic_index_in_dim(by_block, partner, 2, keepdims=False)
            slot_results.append(lag_products(left_channel_block, right_block, 0, LAGS))
        return (jnp.stack(slot_results) / math.sqrt(TIME)).astype(jnp.bfloat16)
    return lax.map(single_owner_rows, jnp.arange(BLOCKS, dtype=jnp.int32))
```

```python
import math

import jax
import jax.numpy as jnp
from jax import lax
from jax.experimental import pallas as pl
from jax.experimental.pallas import tpu as pltpu
from jax.sharding import PartitionSpec as P

DECIM = 5
FILT = 31
MAXLAG = 100
BAND = 4
SLOTS = 2
CB = 128
BLOCKS = 128
TS = 1024
RAW = 40
ROWS = 8
EDGE = 16
SHIFTS = 10
PAIR = 2
STEPS = MAXLAG // (SHIFTS * PAIR)
PAD = TS + 128
REACH = MAXLAG - SHIFTS
WIDE = -(-(TS + REACH) // 8) * 8
CHUNK = 256
VMEM = pl.BlockSpec(memory_space=pltpu.VMEM)
SMEM = pl.BlockSpec(memory_space=pltpu.SMEM)
F32 = jnp.float32
BF16 = jnp.bfloat16


def split3(x):
    parts = []
    for _ in range(3):
        part = x.astype(BF16)
        parts.append(part)
        x = x - part.astype(F32)
    return jnp.concatenate(parts, 0)


def fold3(total):
    return (total[:ROWS] + total[ROWS : 2 * ROWS]) + total[2 * ROWS :]


def inner_kernel(band_ref, own_ref, out_ref):
    band = split3(band_ref[:, EDGE : EDGE + RAW])
    for i in range(BLOCKS * CB // CHUNK):
        at = slice(i * CHUNK, (i + 1) * CHUNK)
        out_ref[:, at] = fold3(jnp.dot(band, own_ref[:, at], preferred_element_type=F32))


def inner_filter(band, own):
    return pl.pallas_call(
        inner_kernel,
        in_specs=[VMEM] * 2,
        out_specs=VMEM,
        out_shape=jax.ShapeDtypeStruct((ROWS, BLOCKS * CB), F32),
        compiler_params=pltpu.CompilerParams(vmem_limit_bytes=24 << 20),
        name="inner_filter",
    )(band, own)


def edge_kernel(band_ref, inner_ref, left_ref, right_ref, out_ref):
    left_band = split3(band_ref[:, :EDGE])
    right_band = split3(band_ref[:, EDGE + RAW :])
    for i in range(BLOCKS * CB // CHUNK):
        at = slice(i * CHUNK, (i + 1) * CHUNK)
        edges = jnp.dot(left_band, left_ref[:, at], preferred_element_type=F32)
        edges += jnp.dot(right_band, right_ref[:, at], preferred_element_type=F32)
        rows = (inner_ref[:, at] + fold3(edges)).astype(BF16)
        for j in range(CHUNK // CB):
            for ahead in range(BAND):
                owner = (i * (CHUNK // CB) + j - ahead) % BLOCKS
                out_ref[owner, ahead] = rows[:, j * CB : (j + 1) * CB]


def edge_filter(band, inner, left, right):
    return pl.pallas_call(
        edge_kernel,
        in_specs=[VMEM] * 4,
        out_specs=VMEM,
        out_shape=jax.ShapeDtypeStruct((BLOCKS, BAND, ROWS, CB), BF16),
        compiler_params=pltpu.CompilerParams(vmem_limit_bytes=24 << 20),
        name="edge_filter",
    )(band, inner, left, right)


def pick_kernel(offsets_ref, all_ref, first_ref, second_ref):
    first_ref[0] = all_ref[:, 0]
    first_ref[1] = all_ref[:, offsets_ref[0, 0]]
    second_ref[0] = all_ref[:, offsets_ref[0, 1]]


def pick(offsets, arrived):
    return pl.pallas_call(
        pick_kernel,
        in_specs=[SMEM, VMEM],
        out_specs=[VMEM, VMEM],
        out_shape=[jax.ShapeDtypeStruct((n, BLOCKS, ROWS, CB), BF16) for n in (2, 1)],
        compiler_params=pltpu.CompilerParams(vmem_limit_bytes=24 << 20),
        name="pick",
    )(offsets, arrived)


def wide_rows(x):
    return x.reshape(TS, CB).astype(F32)


def inverse_spread(x):
    return 1.0 / jnp.sqrt(jnp.sum(x * x, axis=0, keepdims=True) / TS + 1e-6)


def build_left(ahead, x, lhs, column, lpad):
    column[...] = jnp.broadcast_to(inverse_spread(x), (CB, CB)).T * (1.0 / math.sqrt(2 * TS))
    lpad[:, 0:TS] = x.T
    lpad[:, TS:PAD] = jnp.zeros((CB, PAD - TS), F32)
    lpad[...] = pltpu.roll(lpad[...], jnp.where(ahead, 0, PAD - SHIFTS), 1)
    for g in range(SHIFTS):
        moved = lpad[...] if g == 0 else pltpu.roll(lpad[...], g, 1)
        lhs[g * CB : (g + 1) * CB, :] = moved[:, :TS].astype(BF16)


def build_right(ahead, x, win, fac, column, wide):
    fac[...] = column[...] * inverse_spread(x)

    def place(off):
        if off:
            wide[0:off, :] = jnp.zeros((off, CB), F32)
        if off + TS < WIDE:
            wide[off + TS : WIDE, :] = jnp.zeros((WIDE - off - TS, CB), F32)
        wide[off : off + TS, :] = x

    pl.when(ahead)(lambda: place(0))
    pl.when(jnp.logical_not(ahead))(lambda: place(REACH))
    for h in range(STEPS * PAIR):
        at = SHIFTS * h
        k = h % PAIR
        win[h // PAIR, :, k * CB : (k + 1) * CB] = wide[at : at + TS, :].astype(BF16)


def emit(acc, fac, out_ref, add_ref=None):
    for g in range(SHIFTS):
        for k in range(PAIR):
            value = acc[g * CB : (g + 1) * CB, k * CB : (k + 1) * CB] * fac
            if add_ref is not None:
                value += add_ref[0, k * SHIFTS + g]
            out_ref[0, k * SHIFTS + g] = value.astype(out_ref.dtype)


def own_kernel(seg_ref, offsets_ref, all_ref, out_ref, lhs, win, fac, column, wide, lpad, acc):
    step = pl.program_id(0)
    ahead = seg_ref[0] == 1

    @pl.when(step == 0)
    def _():
        build_left(ahead, wide_rows(all_ref[:, 0]), lhs, column, lpad)
        for q in range(SLOTS):
            x = wide_rows(all_ref[:, offsets_ref[0, q]])
            build_right(ahead, x, win.at[pl.ds(q * STEPS, STEPS)], fac.at[q], column, wide)

    acc[...] = jnp.dot(lhs[...], win[step], preferred_element_type=F32)
    emit(acc, fac[step // STEPS], out_ref)


def cost(products):
    return pl.CostEstimate(flops=2 * products * CB * CB * TS, bytes_accessed=8 << 20, transcendentals=0)


def own_products(seg, offsets, arrived):
    return pl.pallas_call(
        own_kernel,
        grid_spec=pltpu.PrefetchScalarGridSpec(
            num_scalar_prefetch=2,
            grid=(SLOTS * STEPS,),
            in_specs=[pl.BlockSpec((BLOCKS, BAND, ROWS, CB), lambda h, s, o: (0, 0, 0, 0))],
            out_specs=pl.BlockSpec((1, PAIR * SHIFTS, CB, CB), lambda h, s, o: (h // STEPS, h % STEPS, 0, 0)),
            scratch_shapes=[
                pltpu.VMEM((SHIFTS * CB, TS), BF16),
                pltpu.VMEM((SLOTS * STEPS, TS, PAIR * CB), BF16),
                pltpu.VMEM((SLOTS, CB, CB), F32),
                pltpu.VMEM((CB, CB), F32),
                pltpu.VMEM((WIDE, CB), F32),
                pltpu.VMEM((CB, PAD), F32),
                pltpu.VMEM((SHIFTS * CB, PAIR * CB), F32),
            ],
        ),
        out_shape=jax.ShapeDtypeStruct((SLOTS, MAXLAG, CB, CB), F32),
        compiler_params=pltpu.CompilerParams(vmem_limit_bytes=32 << 20, dimension_semantics=("arbitrary",)),
        cost_estimate=cost(SLOTS * MAXLAG),
        name="own_products",
    )(seg, offsets, arrived)


def first_kernel(seg_ref, other_ref, own_ref, out_ref, lhs, column, win, fac, wide, lpad, acc):
    step = pl.program_id(0)
    ahead = seg_ref[0] == 1

    @pl.when(step == 0)
    def _():
        build_left(ahead, wide_rows(other_ref[0]), lhs, column, lpad)
        build_right(ahead, wide_rows(other_ref[1]), win, fac, column, wide)

    acc[...] = jnp.dot(lhs[...], win[step], preferred_element_type=F32)
    emit(acc, fac[...], out_ref, own_ref)


def second_kernel(seg_ref, other_ref, lhs, column, own_ref, _, out_ref, win, fac, wide, acc):
    step = pl.program_id(0)

    @pl.when(step == 0)
    def _():
        build_right(seg_ref[0] == 1, wide_rows(other_ref[0]), win, fac, column, wide)

    acc[...] = jnp.dot(lhs[...], win[step], preferred_element_type=F32)
    emit(acc, fac[...], out_ref, own_ref)


def slot_spec(q):
    return pl.BlockSpec((1, PAIR * SHIFTS, CB, CB), lambda h, s: (q, h, 0, 0))


def fixed(*shape):
    return pl.BlockSpec(shape, lambda h, s: (0,) * len(shape))


def first_products(seg, other, own):
    return pl.pallas_call(
        first_kernel,
        grid_spec=pltpu.PrefetchScalarGridSpec(
            num_scalar_prefetch=1,
            grid=(STEPS,),
            in_specs=[fixed(2, BLOCKS, ROWS, CB), slot_spec(0)],
            out_specs=[slot_spec(0), fixed(SHIFTS * CB, TS), fixed(CB, CB)],
            scratch_shapes=[
                pltpu.VMEM((STEPS, TS, PAIR * CB), BF16),
                pltpu.VMEM((CB, CB), F32),
                pltpu.VMEM((WIDE, CB), F32),
                pltpu.VMEM((CB, PAD), F32),
                pltpu.VMEM((SHIFTS * CB, PAIR * CB), F32),
            ],
        ),
        out_shape=[
            jax.ShapeDtypeStruct((SLOTS, MAXLAG, CB, CB), BF16),
            jax.ShapeDtypeStruct((SHIFTS * CB, TS), BF16),
            jax.ShapeDtypeStruct((CB, CB), F32),
        ],
        compiler_params=pltpu.CompilerParams(vmem_limit_bytes=32 << 20, dimension_semantics=("arbitrary",)),
        cost_estimate=cost(MAXLAG),
        name="first_products",
    )(seg, other, own)


def second_products(seg, other, lhs, column, own, lags):
    return pl.pallas_call(
        second_kernel,
        grid_spec=pltpu.PrefetchScalarGridSpec(
            num_scalar_prefetch=1,
            grid=(STEPS,),
            in_specs=[
                fixed(1, BLOCKS, ROWS, CB),
                fixed(SHIFTS * CB, TS),
                fixed(CB, CB),
                slot_spec(1),
                pl.BlockSpec(memory_space=pl.ANY),
            ],
            out_specs=slot_spec(1),
            scratch_shapes=[
                pltpu.VMEM((STEPS, TS, PAIR * CB), BF16),
                pltpu.VMEM((CB, CB), F32),
                pltpu.VMEM((WIDE, CB), F32),
                pltpu.VMEM((SHIFTS * CB, PAIR * CB), F32),
            ],
        ),
        out_shape=jax.ShapeDtypeStruct((SLOTS, MAXLAG, CB, CB), BF16),
        input_output_aliases={5: 0},
        compiler_params=pltpu.CompilerParams(vmem_limit_bytes=32 << 20, dimension_semantics=("arbitrary",)),
        cost_estimate=cost(MAXLAG),
        name="second_products",
    )(seg, other, lhs, column, own, lags)


def banded(filter_taps):
    width = 2 * EDGE + RAW
    rows = [jnp.pad(filter_taps, (1 + DECIM * m, width - 1 - DECIM * m - FILT)) for m in range(ROWS)]
    return jnp.stack(rows)


def on_device(recording, filter_taps, pair_offsets):
    raw = recording[0]
    last = BLOCKS - 1
    left = lax.ppermute(raw[RAW - EDGE :], "blk", [(i, i + 1) for i in range(last)])
    right = lax.ppermute(raw[:EDGE], "blk", [(i + 1, i) for i in range(last)])
    band = banded(filter_taps)
    dealt = edge_filter(band, inner_filter(band, raw), left, right)
    arrived = lax.all_to_all(dealt, "blk", split_axis=0, concat_axis=0, tiled=True)
    seg = lax.axis_index("seg").astype(jnp.int32).reshape(1)
    swap = [(0, 1), (1, 0)]
    first, second = pick(pair_offsets, arrived)
    first = lax.ppermute(first, "seg", swap)
    second = lax.ppermute(second, "seg", swap)
    own = own_products(seg, pair_offsets, arrived)
    lags, lhs, column = first_products(seg, first, own)
    lags = second_products(seg, second, lhs, column, own, lags)
    return jnp.swapaxes(lags, 1, 2)[None]


def solution(mesh):
    placed = (P("seg", "blk", None), P(), P("blk", None))
    return jax.shard_map(
        on_device,
        mesh=mesh,
        in_specs=placed,
        out_specs=P("blk", None, None, "seg", None),
        check_vma=False,
    )
```

```python
import functools
import math

import jax
import jax.numpy as jnp
from jax import lax
from jax.experimental import pallas as pl
from jax.experimental.pallas import tpu as pltpu
from jax.sharding import PartitionSpec as P

DECIM = 5
FILT = 31
MAXLAG = 100
DEALT = (0, 2)
SLOTS = 2
CB = 128
BLOCKS = 128
TS = 1024
RAW = 40
ROWS = 8
EDGE = 16
SHIFTS = 10
PAIR = 2
STEPS = MAXLAG // (SHIFTS * PAIR)
PAD = TS + 128
REACH = MAXLAG - SHIFTS
WIDE = -(-(TS + REACH) // 8) * 8
CHUNK = 256
VMEM = pl.BlockSpec(memory_space=pltpu.VMEM)
SMEM = pl.BlockSpec(memory_space=pltpu.SMEM)
F32 = jnp.float32
BF16 = jnp.bfloat16


def split3(x):
    parts = []
    for _ in range(3):
        part = x.astype(BF16)
        parts.append(part)
        x = x - part.astype(F32)
    return jnp.concatenate(parts, 0)


def fold3(total):
    return (total[:ROWS] + total[ROWS : 2 * ROWS]) + total[2 * ROWS :]


def inner_kernel(band_ref, own_ref, out_ref):
    band = split3(band_ref[:, EDGE : EDGE + RAW])
    for i in range(BLOCKS * CB // CHUNK):
        at = slice(i * CHUNK, (i + 1) * CHUNK)
        out_ref[:, at] = fold3(jnp.dot(band, own_ref[:, at], preferred_element_type=F32))


def inner_filter(band, own):
    return pl.pallas_call(
        inner_kernel,
        in_specs=[VMEM] * 2,
        out_specs=VMEM,
        out_shape=jax.ShapeDtypeStruct((ROWS, BLOCKS * CB), F32),
        compiler_params=pltpu.CompilerParams(vmem_limit_bytes=24 << 20),
        name="inner_filter",
    )(band, own)


def edge_kernel(band_ref, inner_ref, left_ref, right_ref, out_ref):
    left_band = split3(band_ref[:, :EDGE])
    right_band = split3(band_ref[:, EDGE + RAW :])
    for i in range(BLOCKS * CB // CHUNK):
        at = slice(i * CHUNK, (i + 1) * CHUNK)
        edges = jnp.dot(left_band, left_ref[:, at], preferred_element_type=F32)
        edges += jnp.dot(right_band, right_ref[:, at], preferred_element_type=F32)
        rows = (inner_ref[:, at] + fold3(edges)).astype(BF16)
        for j in range(CHUNK // CB):
            for place, ahead in enumerate(DEALT):
                owner = (i * (CHUNK // CB) + j - ahead) % BLOCKS
                out_ref[owner, place] = rows[:, j * CB : (j + 1) * CB]


def edge_filter(band, inner, left, right):
    return pl.pallas_call(
        edge_kernel,
        in_specs=[VMEM] * 4,
        out_specs=VMEM,
        out_shape=jax.ShapeDtypeStruct((BLOCKS, len(DEALT), ROWS, CB), BF16),
        compiler_params=pltpu.CompilerParams(vmem_limit_bytes=24 << 20),
        name="edge_filter",
    )(band, inner, left, right)


BLOCK = jax.ShapeDtypeStruct((BLOCKS, ROWS, CB), BF16)


def part_kernel(odd_ref, arrived_ref, zero_ref, two_ref, pair_ref):
    zero_ref[...] = arrived_ref[:, 0]
    two_ref[...] = arrived_ref[:, 1]
    pair_ref[...] = arrived_ref[:, 1 - odd_ref[0]]


def part(odd, arrived):
    return pl.pallas_call(
        part_kernel,
        in_specs=[SMEM, VMEM],
        out_specs=[VMEM] * 3,
        out_shape=[BLOCK] * 3,
        compiler_params=pltpu.CompilerParams(vmem_limit_bytes=24 << 20),
        name="part",
    )(odd, arrived)


def pick_kernel(q, offsets_ref, *refs):
    for ahead in range(4):

        @pl.when(offsets_ref[0, q] == ahead)
        def _(ahead=ahead):
            refs[-1][...] = refs[ahead][...]


def pick(q, offsets, blocks):
    return pl.pallas_call(
        functools.partial(pick_kernel, q),
        in_specs=[SMEM] + [VMEM] * len(blocks),
        out_specs=VMEM,
        out_shape=BLOCK,
        compiler_params=pltpu.CompilerParams(vmem_limit_bytes=24 << 20),
        name="pick",
    )(offsets, *blocks)


def wide_rows(x):
    return x.reshape(TS, CB).astype(F32)


def inverse_spread(x):
    return 1.0 / jnp.sqrt(jnp.sum(x * x, axis=0, keepdims=True) / TS + 1e-6)


def pad_left(ahead, x, column, lpad):
    column[...] = jnp.broadcast_to(inverse_spread(x), (CB, CB)).T * (1.0 / math.sqrt(2 * TS))
    lpad[:, 0:TS] = x.T
    lpad[:, TS:PAD] = jnp.zeros((CB, PAD - TS), F32)
    lpad[...] = pltpu.roll(lpad[...], jnp.where(ahead, 0, PAD - SHIFTS), 1)


def left_kernel(seg_ref, own_ref, lhs, column, lpad):
    pad_left(seg_ref[0] == 1, wide_rows(own_ref[...]), column, lpad)
    for g in range(SHIFTS):
        moved = lpad[...] if g == 0 else pltpu.roll(lpad[...], g, 1)
        lhs[g * CB : (g + 1) * CB, :] = moved[:, :TS].astype(BF16)


LEFT = [jax.ShapeDtypeStruct((SHIFTS * CB, TS), BF16), jax.ShapeDtypeStruct((CB, CB), F32)]


def left_rows(seg, own):
    return pl.pallas_call(
        left_kernel,
        in_specs=[SMEM, VMEM],
        out_specs=[VMEM] * 2,
        out_shape=LEFT,
        scratch_shapes=[pltpu.VMEM((CB, PAD), F32)],
        compiler_params=pltpu.CompilerParams(vmem_limit_bytes=24 << 20),
        cost_estimate=pl.CostEstimate(flops=1 << 20, bytes_accessed=9 << 20, transcendentals=0),
        name="left_rows",
    )(seg, own)


def build_right(ahead, x, win, fac, column, wide):
    fac[...] = column[...] * inverse_spread(x)

    def place(off):
        if off:
            wide[0:off, :] = jnp.zeros((off, CB), F32)
        if off + TS < WIDE:
            wide[off + TS : WIDE, :] = jnp.zeros((WIDE - off - TS, CB), F32)
        wide[off : off + TS, :] = x

    pl.when(ahead)(lambda: place(0))
    pl.when(jnp.logical_not(ahead))(lambda: place(REACH))
    for h in range(STEPS * PAIR):
        at = SHIFTS * h
        k = h % PAIR
        win[h // PAIR, :, k * CB : (k + 1) * CB] = wide[at : at + TS, :].astype(BF16)


def own_kernel(seg_ref, lhs, column, right0_ref, right1_ref, out_ref, fac, win, wide):
    ahead = seg_ref[0] == 1
    for q, ref in enumerate((right0_ref, right1_ref)):
        build_right(ahead, wide_rows(ref[...]), win.at[pl.ds(q * STEPS, STEPS)], fac.at[q], column, wide)

    def multiply(step, carry):
        out_ref[step] = jnp.dot(lhs[...], win[step], preferred_element_type=F32)
        return carry

    lax.fori_loop(0, SLOTS * STEPS, multiply, 0, unroll=5)


def cost(products):
    return pl.CostEstimate(flops=2 * products * CB * CB * TS, bytes_accessed=8 << 20, transcendentals=0)


def slot_spec(q):
    return pl.BlockSpec((1, PAIR * SHIFTS, CB, CB), lambda h, s: (q, h, 0, 0))


def fixed(*shape):
    return pl.BlockSpec(shape, lambda h, s: (0,) * len(shape))


def own_products(seg, lhs, column, rights):
    return pl.pallas_call(
        own_kernel,
        in_specs=[SMEM] + [VMEM] * 4,
        out_specs=[VMEM] * 2,
        out_shape=[
            jax.ShapeDtypeStruct((SLOTS * STEPS, SHIFTS * CB, PAIR * CB), F32),
            jax.ShapeDtypeStruct((SLOTS, CB, CB), F32),
        ],
        scratch_shapes=[
            pltpu.VMEM((SLOTS * STEPS, TS, PAIR * CB), BF16),
            pltpu.VMEM((WIDE, CB), F32),
        ],
        compiler_params=pltpu.CompilerParams(vmem_limit_bytes=28 << 20),
        cost_estimate=cost(SLOTS * MAXLAG),
        name="own_products",
    )(seg, lhs, column, *rights)


def other_kernel(seg_ref, other_ref, lhs, column, own_ref, own_fac, *refs):
    out_ref, win, fac, wide, acc = refs[-5:]
    step = pl.program_id(0)

    @pl.when(step == 0)
    def _():
        build_right(seg_ref[0] == 1, wide_rows(other_ref[...]), win, fac, column, wide)

    acc[...] = jnp.dot(lhs[...], win[step], preferred_element_type=F32)
    for g in range(SHIFTS):
        for k in range(PAIR):
            at = slice(g * CB, (g + 1) * CB), slice(k * CB, (k + 1) * CB)
            value = acc[at] * fac[...] + own_ref[(0,) + at] * own_fac[0]
            out_ref[0, k * SHIFTS + g] = value.astype(BF16)


def other_products(q, seg, other, lhs, column, own, lags):
    return pl.pallas_call(
        other_kernel,
        grid_spec=pltpu.PrefetchScalarGridSpec(
            num_scalar_prefetch=1,
            grid=(STEPS,),
            in_specs=[
                fixed(BLOCKS, ROWS, CB),
                fixed(SHIFTS * CB, TS),
                fixed(CB, CB),
                pl.BlockSpec((1, SHIFTS * CB, PAIR * CB), lambda h, s: (q * STEPS + h, 0, 0)),
                pl.BlockSpec((1, CB, CB), lambda h, s: (q, 0, 0)),
            ]
            + [pl.BlockSpec(memory_space=pl.ANY)] * len(lags),
            out_specs=slot_spec(q),
            scratch_shapes=[
                pltpu.VMEM((STEPS, TS, PAIR * CB), BF16),
                pltpu.VMEM((CB, CB), F32),
                pltpu.VMEM((WIDE, CB), F32),
                pltpu.VMEM((SHIFTS * CB, PAIR * CB), F32),
            ],
        ),
        out_shape=jax.ShapeDtypeStruct((SLOTS, MAXLAG, CB, CB), BF16),
        input_output_aliases={6: 0} if lags else {},
        compiler_params=pltpu.CompilerParams(vmem_limit_bytes=28 << 20, dimension_semantics=("arbitrary",)),
        cost_estimate=cost(MAXLAG),
        name="other_products",
    )(seg, other, lhs, column, *own, *lags)


def banded(filter_taps):
    width = 2 * EDGE + RAW
    rows = [jnp.pad(filter_taps, (1 + DECIM * m, width - 1 - DECIM * m - FILT)) for m in range(ROWS)]
    return jnp.stack(rows)


def on_device(recording, filter_taps, pair_offsets):
    raw = recording[0]
    last = BLOCKS - 1
    left = lax.ppermute(raw[RAW - EDGE :], "blk", [(i, i + 1) for i in range(last)])
    right = lax.ppermute(raw[:EDGE], "blk", [(i + 1, i) for i in range(last)])
    band = banded(filter_taps)
    dealt = edge_filter(band, inner_filter(band, raw), left, right)
    arrived = lax.all_to_all(dealt, "blk", split_axis=0, concat_axis=0, tiled=True)
    seg = lax.axis_index("seg").astype(jnp.int32).reshape(1)
    odd = (lax.axis_index("blk") % 2).astype(jnp.int32).reshape(1)
    swap = [(0, 1), (1, 0)]
    zero, two, pair = part(odd, arrived)
    one = lax.ppermute(pair, "blk", [(i, i ^ 1) for i in range(BLOCKS)])
    three = lax.ppermute(two, "blk", [(i, (i - 1) % BLOCKS) for i in range(BLOCKS)])
    other_left = lax.ppermute(zero, "seg", swap)
    lhs, column = left_rows(seg, zero)
    blocks = (zero, one, two, three)
    right = pick(0, pair_offsets, blocks)
    rights = (right, pick(1, pair_offsets, (*blocks, right)))
    other_rights = [lax.ppermute(right, "seg", swap) for right in rights]
    own = own_products(seg, lhs, column, rights)
    *own, other_left = lax.optimization_barrier((*own, other_left))
    other_lhs, other_column = left_rows(seg, other_left)
    lags = []
    for q in range(SLOTS):
        lags = [other_products(q, seg, other_rights[q], other_lhs, other_column, own, lags)]
    return jnp.swapaxes(lags[0], 1, 2)[None]


def solution(mesh):
    placed = (P("seg", "blk", None), P(), P("blk", None))
    return jax.shard_map(
        on_device,
        mesh=mesh,
        in_specs=placed,
        out_specs=P("blk", None, None, "seg", None),
        check_vma=False,
    )
```

```python
import functools
import math

import jax
import jax.numpy as jnp
from jax import lax
from jax.experimental import pallas as pl
from jax.experimental.pallas import tpu as pltpu
from jax.sharding import PartitionSpec as P

DECIM = 5
FILT = 31
MAXLAG = 100
DEALT = (0, 2)
SLOTS = 2
CB = 128
BLOCKS = 128
TS = 1024
RAW = 40
ROWS = 8
EDGE = 4
SHIFTS = 10
PAIR = 2
STEPS = MAXLAG // (SHIFTS * PAIR)
PAD = TS + 128
REACH = MAXLAG - SHIFTS
WIDE = -(-(TS + REACH) // 8) * 8
CHUNK = 256
VMEM = pl.BlockSpec(memory_space=pltpu.VMEM)
SMEM = pl.BlockSpec(memory_space=pltpu.SMEM)
F32 = jnp.float32
BF16 = jnp.bfloat16


def split3(x):
    parts = []
    for _ in range(3):
        part = x.astype(BF16)
        parts.append(part)
        x = x - part.astype(F32)
    return jnp.concatenate(parts, 0)


def inner_kernel(band_ref, own_ref, inner_ref, to_left_ref, to_right_ref):
    band = split3(band_ref[...])
    count = band_ref.shape[0]
    for i in range(BLOCKS * CB // CHUNK):
        at = slice(i * CHUNK, (i + 1) * CHUNK)
        total = jnp.dot(band, own_ref[:, at], preferred_element_type=F32)
        total = (total[:count] + total[count : 2 * count]) + total[2 * count :]
        inner_ref[:, at] = total[:ROWS]
        to_left_ref[:, at] = total[ROWS : ROWS + EDGE]
        to_right_ref[:, at] = total[ROWS + EDGE :]


def inner_filter(band, own):
    return pl.pallas_call(
        inner_kernel,
        in_specs=[VMEM] * 2,
        out_specs=[VMEM] * 3,
        out_shape=[jax.ShapeDtypeStruct((n, BLOCKS * CB), F32) for n in (ROWS, EDGE, EDGE)],
        compiler_params=pltpu.CompilerParams(vmem_limit_bytes=24 << 20),
        name="inner_filter",
    )(band, own)


def edge_kernel(inner_ref, left_ref, right_ref, out_ref):
    for i in range(BLOCKS):
        at = slice(i * CB, (i + 1) * CB)
        edges = jnp.concatenate([left_ref[:, at], right_ref[:, at]], 0)
        rows = (inner_ref[:, at] + edges).astype(BF16)
        for place, ahead in enumerate(DEALT):
            out_ref[(i - ahead) % BLOCKS, place] = rows


def edge_filter(inner, left, right):
    return pl.pallas_call(
        edge_kernel,
        in_specs=[VMEM] * 3,
        out_specs=VMEM,
        out_shape=jax.ShapeDtypeStruct((BLOCKS, len(DEALT), ROWS, CB), BF16),
        compiler_params=pltpu.CompilerParams(vmem_limit_bytes=24 << 20),
        name="edge_filter",
    )(inner, left, right)


BLOCK = jax.ShapeDtypeStruct((BLOCKS, ROWS, CB), BF16)


def part_kernel(odd_ref, arrived_ref, zero_ref, two_ref, pair_ref):
    zero_ref[...] = arrived_ref[:, 0]
    two_ref[...] = arrived_ref[:, 1]
    pair_ref[...] = arrived_ref[:, 1 - odd_ref[0]]


def part(odd, arrived):
    return pl.pallas_call(
        part_kernel,
        in_specs=[SMEM, VMEM],
        out_specs=[VMEM] * 3,
        out_shape=[BLOCK] * 3,
        compiler_params=pltpu.CompilerParams(vmem_limit_bytes=24 << 20),
        name="part",
    )(odd, arrived)


def pick_kernel(q, offsets_ref, *refs):
    for ahead in range(4):

        @pl.when(offsets_ref[0, q] == ahead)
        def _(ahead=ahead):
            refs[-1][...] = refs[ahead][...]


def pick(q, offsets, blocks):
    return pl.pallas_call(
        functools.partial(pick_kernel, q),
        in_specs=[SMEM] + [VMEM] * len(blocks),
        out_specs=VMEM,
        out_shape=BLOCK,
        compiler_params=pltpu.CompilerParams(vmem_limit_bytes=24 << 20),
        name="pick",
    )(offsets, *blocks)


def wide_rows(x):
    return x.reshape(TS, CB).astype(F32)


def inverse_spread(x):
    return 1.0 / jnp.sqrt(jnp.sum(x * x, axis=0, keepdims=True) / TS + 1e-6)


def pad_left(ahead, x, column, lpad):
    column[...] = jnp.broadcast_to(inverse_spread(x), (CB, CB)).T * (1.0 / math.sqrt(2 * TS))
    lpad[:, 0:TS] = x.T
    lpad[:, TS:PAD] = jnp.zeros((CB, PAD - TS), F32)
    lpad[...] = pltpu.roll(lpad[...], jnp.where(ahead, 0, PAD - SHIFTS), 1)


def left_kernel(seg_ref, own_ref, lhs, column, lpad):
    pad_left(seg_ref[0] == 1, wide_rows(own_ref[...]), column, lpad)
    for g in range(SHIFTS):
        moved = lpad[...] if g == 0 else pltpu.roll(lpad[...], g, 1)
        lhs[g * CB : (g + 1) * CB, :] = moved[:, :TS].astype(BF16)


LEFT = [jax.ShapeDtypeStruct((SHIFTS * CB, TS), BF16), jax.ShapeDtypeStruct((CB, CB), F32)]


def left_rows(seg, own):
    return pl.pallas_call(
        left_kernel,
        in_specs=[SMEM, VMEM],
        out_specs=[VMEM] * 2,
        out_shape=LEFT,
        scratch_shapes=[pltpu.VMEM((CB, PAD), F32)],
        compiler_params=pltpu.CompilerParams(vmem_limit_bytes=24 << 20),
        cost_estimate=pl.CostEstimate(flops=1 << 20, bytes_accessed=9 << 20, transcendentals=0),
        name="left_rows",
    )(seg, own)


def build_right(ahead, x, win, fac, column, wide):
    fac[...] = column[...] * inverse_spread(x)

    def place(off):
        if off:
            wide[0:off, :] = jnp.zeros((off, CB), F32)
        if off + TS < WIDE:
            wide[off + TS : WIDE, :] = jnp.zeros((WIDE - off - TS, CB), F32)
        wide[off : off + TS, :] = x

    pl.when(ahead)(lambda: place(0))
    pl.when(jnp.logical_not(ahead))(lambda: place(REACH))
    for h in range(STEPS * PAIR):
        at = SHIFTS * h
        k = h % PAIR
        win[h // PAIR, :, k * CB : (k + 1) * CB] = wide[at : at + TS, :].astype(BF16)


def own_kernel(seg_ref, lhs, column, right0_ref, right1_ref, out_ref, fac, win, wide):
    ahead = seg_ref[0] == 1
    for q, ref in enumerate((right0_ref, right1_ref)):
        build_right(ahead, wide_rows(ref[...]), win.at[pl.ds(q * STEPS, STEPS)], fac.at[q], column, wide)

    def multiply(step, carry):
        out_ref[step] = jnp.dot(lhs[...], win[step], preferred_element_type=F32)
        return carry

    lax.fori_loop(0, SLOTS * STEPS, multiply, 0, unroll=5)


def cost(products):
    return pl.CostEstimate(flops=2 * products * CB * CB * TS, bytes_accessed=8 << 20, transcendentals=0)


def slot_spec(q):
    return pl.BlockSpec((1, PAIR * SHIFTS, CB, CB), lambda h, s: (q, h, 0, 0))


def fixed(*shape):
    return pl.BlockSpec(shape, lambda h, s: (0,) * len(shape))


def own_products(seg, lhs, column, rights):
    return pl.pallas_call(
        own_kernel,
        in_specs=[SMEM] + [VMEM] * 4,
        out_specs=[VMEM] * 2,
        out_shape=[
            jax.ShapeDtypeStruct((SLOTS * STEPS, SHIFTS * CB, PAIR * CB), F32),
            jax.ShapeDtypeStruct((SLOTS, CB, CB), F32),
        ],
        scratch_shapes=[
            pltpu.VMEM((SLOTS * STEPS, TS, PAIR * CB), BF16),
            pltpu.VMEM((WIDE, CB), F32),
        ],
        compiler_params=pltpu.CompilerParams(vmem_limit_bytes=28 << 20),
        cost_estimate=cost(SLOTS * MAXLAG),
        name="own_products",
    )(seg, lhs, column, *rights)


def other_kernel(seg_ref, other_ref, lhs, column, own_ref, own_fac, *refs):
    out_ref, win, fac, wide, acc = refs[-5:]
    step = pl.program_id(0)

    @pl.when(step == 0)
    def _():
        build_right(seg_ref[0] == 1, wide_rows(other_ref[...]), win, fac, column, wide)

    acc[...] = jnp.dot(lhs[...], win[step], preferred_element_type=F32)
    for g in range(SHIFTS):
        for k in range(PAIR):
            at = slice(g * CB, (g + 1) * CB), slice(k * CB, (k + 1) * CB)
            value = acc[at] * fac[...] + own_ref[(0,) + at] * own_fac[0]
            out_ref[0, k * SHIFTS + g] = value.astype(BF16)


def other_products(q, seg, other, lhs, column, own, lags):
    return pl.pallas_call(
        other_kernel,
        grid_spec=pltpu.PrefetchScalarGridSpec(
            num_scalar_prefetch=1,
            grid=(STEPS,),
            in_specs=[
                fixed(BLOCKS, ROWS, CB),
                fixed(SHIFTS * CB, TS),
                fixed(CB, CB),
                pl.BlockSpec((1, SHIFTS * CB, PAIR * CB), lambda h, s: (q * STEPS + h, 0, 0)),
                pl.BlockSpec((1, CB, CB), lambda h, s: (q, 0, 0)),
            ]
            + [pl.BlockSpec(memory_space=pl.ANY)] * len(lags),
            out_specs=slot_spec(q),
            scratch_shapes=[
                pltpu.VMEM((STEPS, TS, PAIR * CB), BF16),
                pltpu.VMEM((CB, CB), F32),
                pltpu.VMEM((WIDE, CB), F32),
                pltpu.VMEM((SHIFTS * CB, PAIR * CB), F32),
            ],
        ),
        out_shape=jax.ShapeDtypeStruct((SLOTS, MAXLAG, CB, CB), BF16),
        input_output_aliases={6: 0} if lags else {},
        compiler_params=pltpu.CompilerParams(vmem_limit_bytes=28 << 20, dimension_semantics=("arbitrary",)),
        cost_estimate=cost(MAXLAG),
        name="other_products",
    )(seg, other, lhs, column, *own, *lags)


def banded(filter_taps):
    blank = jnp.zeros((RAW,), filter_taps.dtype)

    def row(m):
        first = DECIM * m - FILT // 2
        start = max(0, -first)
        stop = min(FILT, RAW - first)
        return jnp.pad(filter_taps[start:stop], (first + start, RAW - first - stop))

    rows = [row(m) for m in range(ROWS)]
    rows += [blank] + [row(m) for m in (-3, -2, -1)]
    rows += [row(ROWS + m) for m in range(3)] + [blank]
    return jnp.stack(rows)


def on_device(recording, filter_taps, pair_offsets):
    raw = recording[0]
    last = BLOCKS - 1
    inner, to_left, to_right = inner_filter(banded(filter_taps), raw)
    left = lax.ppermute(to_right, "blk", [(i, i + 1) for i in range(last)])
    right = lax.ppermute(to_left, "blk", [(i + 1, i) for i in range(last)])
    dealt = edge_filter(inner, left, right)
    arrived = lax.all_to_all(dealt, "blk", split_axis=0, concat_axis=0, tiled=True)
    seg = lax.axis_index("seg").astype(jnp.int32).reshape(1)
    odd = (lax.axis_index("blk") % 2).astype(jnp.int32).reshape(1)
    swap = [(0, 1), (1, 0)]
    zero, two, pair = part(odd, arrived)
    one = lax.ppermute(pair, "blk", [(i, i ^ 1) for i in range(BLOCKS)])
    three = lax.ppermute(two, "blk", [(i, (i - 1) % BLOCKS) for i in range(BLOCKS)])
    other_left = lax.ppermute(zero, "seg", swap)
    lhs, column = left_rows(seg, zero)
    blocks = (zero, one, two, three)
    right = pick(0, pair_offsets, blocks)
    rights = (right, pick(1, pair_offsets, (*blocks, right)))
    other_rights = [lax.ppermute(right, "seg", swap) for right in rights]
    own = own_products(seg, lhs, column, rights)
    *own, other_left = lax.optimization_barrier((*own, other_left))
    other_lhs, other_column = left_rows(seg, other_left)
    lags = []
    for q in range(SLOTS):
        lags = [other_products(q, seg, other_rights[q], other_lhs, other_column, own, lags)]
    return jnp.swapaxes(lags[0], 1, 2)[None]


def solution(mesh):
    placed = (P("seg", "blk", None), P(), P("blk", None))
    return jax.shard_map(
        on_device,
        mesh=mesh,
        in_specs=placed,
        out_specs=P("blk", None, None, "seg", None),
        check_vma=False,
    )
```
